32 devices in a mesh: dp: 2 (over x), space: 16 (over z, y, core).
Axes of the slice: x: 2, y: 2, z: 4, core: 2. Of those that a mesh axis runs over, the one named last changes fastest.
Arguments:
- activations: bfloat16 [4, 16, 64, 256], P('dp', 'space'), may hold values from -6 to 6
- out_grads: bfloat16 [4, 16, 64, 256], P('dp', 'space'), may hold values from -6 to 6
- old_input_factor: bfloat16 [2304, 2304], P(('dp', 'space')), may hold values from -3 to 3
- old_grad_factor: float32 [256, 256], P('space'), may hold values from -3 to 3
Outputs:
- input_factor: float32 [2304, 2304], P(('dp', 'space'))
- grad_factor: float32 [256, 256], P('space')
The draws below stay inside these ranges and needn't reach their ends.
All inputs are finite; a program needn't handle non-finite values.
Results may differ from the reference program's by a relative error of at most 0.00055.
Values may be sent and summed in bfloat16 or wider, within the bound.
A program may use at most 128 MiB of HBM per device.

```python
import jax
import jax.numpy as jnp
from jax import lax

C = 256
KK = 2304
WIDTH = 64
BATCH = 4
HEIGHT = 16


def raised(entries, own_key, source, target, blocks, factor):
    def block_of(position):
        return (jnp.arange(entries.shape[position]) // (entries.shape[position] // blocks)).reshape((-1,) + (1,) * (entries.ndim - 1 - position))

    one_side = jax.random.permutation(own_key, blocks)[block_of(target)]
    far = (block_of(target) + blocks // 2) % blocks
    return jnp.where((block_of(source) == one_side) | (block_of(source) == far), factor * entries, entries)


def level_of(own_key, shape, split, low, high):
    def one(axis_at, blocks):
        heights = jax.random.uniform(jax.random.fold_in(jax.random.fold_in(own_key, 6), axis_at), (blocks,), jnp.float32, low / len(split), high / len(split))
        return jnp.repeat(jnp.exp(heights), shape[axis_at] // blocks).reshape((-1,) + (1,) * (len(shape) - axis_at - 1))

    gain = one(*split[0])
    for cut in split[1:]:
        gain = gain * one(*cut)
    return gain


def centred(stream_key, dims, spread, limit, shards=(), kind=jnp.bfloat16):
    array = spread * jax.random.normal(stream_key, dims, jnp.float32)
    if shards:
        array = array * level_of(stream_key, dims, shards, -0.22, 0.18)
    return jnp.clip(array, -limit, limit).astype(kind)


def noise_with(stream_key, dims, scale, limit, cuts, heavy, dtype=jnp.bfloat16):
    entries = scale * jax.random.normal(stream_key, dims, jnp.float32)
    if cuts:
        entries = entries * level_of(stream_key, dims, cuts, -0.22, 0.18)
    return jnp.clip(raised(entries, jax.random.fold_in(stream_key, 3), *heavy), -limit, limit).astype(dtype)


def setup_inputs(seed: int = 0) -> dict:
    arg_keys = jax.random.split(jax.random.key(seed), 5)
    return {
        "activations": noise_with(arg_keys[0], (BATCH, HEIGHT, WIDTH, C), 1.0, 6.0, ((0, 2), (1, 16)), (1, 3, 16, 2.0)),
        "out_grads": noise_with(arg_keys[1], (BATCH, HEIGHT, WIDTH, C), 1.0, 6.0, ((0, 2), (1, 16)), (1, 3, 16, 2.0)),
        "old_input_factor": centred(arg_keys[2], (KK, KK), 0.5, 3.0, ((0, 32),)),
        "old_grad_factor": centred(arg_keys[3], (C, C), 0.5, 3.0, ((0, 16),), jnp.float32),
    }


def patch_rows(image):
    height_now, width_now = image.shape[0], image.shape[1]
    padded = jnp.pad(image, ((1, 1), (1, 1), (0, 0)))
    pieces = [padded[ky:ky + height_now, kx:kx + width_now, :] for ky in range(3) for kx in range(3)]
    return jnp.concatenate(pieces, axis=2).reshape(height_now * width_now, -1)


def reference(activations, out_grads, old_input_factor, old_grad_factor):
    def step(carry, pair):
        image, grad_image = pair
        patches = patch_rows(image)
        flat = grad_image.reshape(-1, grad_image.shape[-1])
        input_part = lax.dot_general(patches, patches, (((0,), (0,)), ((), ())), preferred_element_type=jnp.float32)
        grad_part = lax.dot_general(flat, flat, (((0,), (0,)), ((), ())), preferred_element_type=jnp.float32)
        return (carry[0] + input_part, carry[1] + grad_part), None

    start = (jnp.zeros(old_input_factor.shape, jnp.float32), jnp.zeros(old_grad_factor.shape, jnp.float32))
    (input_sum, grad_sum), _ = lax.scan(step, start, (activations, out_grads))
    positions = activations.shape[0] * activations.shape[1] * activations.shape[2]
    input_factor = 0.5 * old_input_factor.astype(jnp.float32) + (0.5 / positions) * input_sum
    grad_factor = 0.5 * old_grad_factor + (0.5 / positions) * grad_sum
    return input_factor, grad_factor
```

```python
import jax
import jax.numpy as jnp
from jax import lax
from jax.sharding import PartitionSpec as P


def extended(block, sides, width):
    for axis, dim in sides:
        count = lax.axis_size(axis)
        forward = [(i, i + 1) for i in range(count - 1)]
        backward = [(target, source) for source, target in forward]
        low = lax.ppermute(
            lax.slice_in_dim(block, block.shape[dim] - width, None, axis=dim), axis, forward
        )
        high = lax.ppermute(lax.slice_in_dim(block, 0, width, axis=dim), axis, backward)
        block = jnp.concatenate([low, block, high], axis=dim)
    return block


def transposed_product(left, right):
    return lax.dot_general(
        left, right, (((0,), (0,)), ((), ())), preferred_element_type=jnp.float32
    )


def reduced_form(activations, out_grads, old_input_factor, old_grad_factor):
    images, rows_here, columns_here, channels = activations.shape
    widened = extended(activations, (("space", 1),), 1)
    padded = jnp.pad(widened, ((0, 0), (0, 0), (1, 1), (0, 0)))
    pieces = [
        padded[:, ky : ky + rows_here, kx : kx + columns_here, :]
        for ky in range(3)
        for kx in range(3)
    ]
    patches = jnp.concatenate(pieces, axis=3).reshape(
        images * rows_here * columns_here, 9 * channels
    )
    groups = lax.axis_size("dp")
    spaces = lax.axis_size("space")
    positions = images * groups * rows_here * spaces * columns_here
    share = old_input_factor.shape[0]
    width_all = patches.shape[1]
    column_blocks = 4
    block_width = width_all // column_blocks
    results = []
    block = share * groups
    for which in range(column_blocks):
        right = patches[:, which * block_width : (which + 1) * block_width]

        def mapped_block(start, count, right=right):
            offsets = jnp.arange(count, dtype=jnp.int32)
            holder_space = offsets // block
            within_block = offsets % block
            holder_group = within_block // share
            within = within_block % share
            columns = holder_group * (spaces * share) + holder_space * share + within
            left = jnp.take(patches, columns, axis=1)
            return transposed_product(left, right)

        results.append(
            lax.psum_scatter(
                mapped_block(jnp.int32(0), block * lax.axis_size("space")),
                "space",
                scatter_dimension=0,
                tiled=True,
            )
        )
    part_sum = jnp.concatenate(results, axis=1)
    input_sum = lax.psum_scatter(
        part_sum.astype(jnp.bfloat16), "dp", scatter_dimension=0, tiled=True
    ).astype(jnp.float32)
    flat_grads = out_grads.reshape(images * rows_here * columns_here, channels)
    grad_term = transposed_product(flat_grads, flat_grads)
    grad_rows_here = old_grad_factor.shape[0]
    grad_total = lax.psum(grad_term, ("dp", "space"))
    grad_sum = lax.dynamic_slice_in_dim(
        grad_total, lax.axis_index("space") * grad_rows_here, grad_rows_here, 0
    )
    input_factor = 0.5 * old_input_factor.astype(jnp.float32) + 0.5 / positions * input_sum
    grad_factor = 0.5 * old_grad_factor + 0.5 / positions * grad_sum
    return (input_factor, grad_factor)


def gathered_form(activations, out_grads, old_input_factor, old_grad_factor):
    images, rows_here, columns, channels = activations.shape
    groups = lax.axis_size("dp")
    spaces = lax.axis_size("space")
    positions = images * groups * rows_here * spaces * columns
    share = old_input_factor.shape[0]
    grad_share = old_grad_factor.shape[0]
    me = lax.axis_index("dp") * spaces + lax.axis_index("space")

    gathered = lax.all_gather(activations, ("dp", "space"), axis=0, tiled=False)
    gathered = gathered.reshape(groups, spaces, images, rows_here, columns, channels)
    full = gathered.transpose(0, 2, 1, 3, 4, 5).reshape(
        groups * images, spaces * rows_here, columns, channels
    )
    height = spaces * rows_here
    padded = jnp.pad(full, ((0, 0), (1, 1), (1, 1), (0, 0)))

    def tap(number):
        return lax.dynamic_slice(
            padded,
            (0, number // 3, number % 3, 0),
            (groups * images, height, columns, channels),
        ).reshape(positions, channels)

    first = me * share
    tap_first = first // channels
    tap_next = jnp.minimum(tap_first + 1, 8)
    both = jnp.concatenate([tap(tap_first), tap(tap_next)], axis=1)
    left = lax.dynamic_slice_in_dim(both, first % channels, share, axis=1)
    sums = []
    for number in range(9):
        right = tap(number)
        sums.append(
            lax.dot_general(
                left, right, (((0,), (0,)), ((), ())), preferred_element_type=jnp.float32
            )
        )
    input_sum = jnp.concatenate(sums, axis=1)
    input_factor = 0.5 * old_input_factor.astype(jnp.float32) + 0.5 / positions * input_sum

    flat = out_grads.reshape(-1, channels)
    grad_term = lax.dot_general(
        flat, flat, (((0,), (0,)), ((), ())), preferred_element_type=jnp.float32
    )
    grad_total = lax.psum(grad_term, ("dp", "space"))
    grad_sum = lax.dynamic_slice_in_dim(
        grad_total, lax.axis_index("space") * grad_share, grad_share, 0
    )
    grad_factor = 0.5 * old_grad_factor + 0.5 / positions * grad_sum
    return input_factor, grad_factor


def per_device(activations, out_grads, old_input_factor, old_grad_factor):
    devices = lax.axis_size("dp") * lax.axis_size("space")
    whole_map = activations.size * devices
    form = gathered_form if whole_map <= old_input_factor.shape[1] ** 2 else reduced_form
    return form(activations, out_grads, old_input_factor, old_grad_factor)


def solution(mesh):
    return jax.shard_map(
        per_device,
        mesh=mesh,
        in_specs=(
            P("dp", "space", None, None),
            P("dp", "space", None, None),
            P(("dp", "space"), None),
            P("space", None),
        ),
        out_specs=(P(("dp", "space"), None), P("space", None)),
        check_vma=False,
    )
```

```python
import jax
import jax.numpy as jnp
from jax import lax
from jax.experimental import pallas as pl
from jax.experimental.pallas import tpu as pltpu
from jax.sharding import PartitionSpec as P


def extended(block, sides, width):
    for axis, dim in sides:
        count = lax.axis_size(axis)
        forward = [(i, i + 1) for i in range(count - 1)]
        backward = [(target, source) for source, target in forward]
        low = lax.ppermute(
            lax.slice_in_dim(block, block.shape[dim] - width, None, axis=dim), axis, forward
        )
        high = lax.ppermute(lax.slice_in_dim(block, 0, width, axis=dim), axis, backward)
        block = jnp.concatenate([low, block, high], axis=dim)
    return block


def transposed_product(left, right):
    return lax.dot_general(
        left, right, (((0,), (0,)), ((), ())), preferred_element_type=jnp.float32
    )


def reduced_form(activations, out_grads, old_input_factor, old_grad_factor):
    images, rows_here, columns_here, channels = activations.shape
    widened = extended(activations, (("space", 1),), 1)
    padded = jnp.pad(widened, ((0, 0), (0, 0), (1, 1), (0, 0)))
    pieces = [
        padded[:, ky : ky + rows_here, kx : kx + columns_here, :]
        for ky in range(3)
        for kx in range(3)
    ]
    patches = jnp.concatenate(pieces, axis=3).reshape(
        images * rows_here * columns_here, 9 * channels
    )
    groups = lax.axis_size("dp")
    spaces = lax.axis_size("space")
    positions = images * groups * rows_here * spaces * columns_here
    share = old_input_factor.shape[0]
    width_all = patches.shape[1]
    column_blocks = 4
    block_width = width_all // column_blocks
    results = []
    block = share * groups
    for which in range(column_blocks):
        right = patches[:, which * block_width : (which + 1) * block_width]

        def mapped_block(start, count, right=right):
            offsets = jnp.arange(count, dtype=jnp.int32)
            holder_space = offsets // block
            within_block = offsets % block
            holder_group = within_block // share
            within = within_block % share
            columns = holder_group * (spaces * share) + holder_space * share + within
            left = jnp.take(patches, columns, axis=1)
            return transposed_product(left, right)

        results.append(
            lax.psum_scatter(
                mapped_block(jnp.int32(0), block * lax.axis_size("space")),
                "space",
                scatter_dimension=0,
                tiled=True,
            )
        )
    part_sum = jnp.concatenate(results, axis=1)
    input_sum = lax.psum_scatter(
        part_sum.astype(jnp.bfloat16), "dp", scatter_dimension=0, tiled=True
    ).astype(jnp.float32)
    flat_grads = out_grads.reshape(images * rows_here * columns_here, channels)
    grad_term = transposed_product(flat_grads, flat_grads)
    grad_rows_here = old_grad_factor.shape[0]
    grad_total = lax.psum(grad_term, ("dp", "space"))
    grad_sum = lax.dynamic_slice_in_dim(
        grad_total, lax.axis_index("space") * grad_rows_here, grad_rows_here, 0
    )
    input_factor = 0.5 * old_input_factor.astype(jnp.float32) + 0.5 / positions * input_sum
    grad_factor = 0.5 * old_grad_factor + 0.5 / positions * grad_sum
    return (input_factor, grad_factor)


MESH = pl.DeviceIdType.MESH
TAPS = 3


def gather_kernel(act, grad, sums, grad_sum, maps, acc, gbuf, gpart, grecv,
                  sz, rz, sx, rx, sy, ry, sdx, rdx, sdy, rdy, sp, rp, sg, rg, ss, rs):
    images, rows, columns, channels = act.shape
    share = sums.shape[0]
    height = maps.shape[1] - 2
    spaces = height // rows
    lines = spaces // 4
    x = lax.axis_index("dp")
    space = lax.axis_index("space")
    core = space % 2
    y = (space // 2) % 2
    z = space // 4
    half = z // 2
    order = [z, z + 1 - 2 * (z % 2), 2 - half, 3 - 3 * half]
    x_other, y_other = 1 - x, 1 - y

    def place(line, yy, kk):
        return line * 4 + yy * 2 + kk

    to_x = (x_other, space)
    to_y = (x, place(z, y_other, core))
    to_p = (x, place(z, y, 1 - core))
    to_grad = [(line, flip) for flip in range(2) for line in range(lines)]

    barrier = pltpu.get_barrier_semaphore()
    pl.semaphore_signal(barrier, inc=1, device_id=to_x, device_id_type=MESH)
    pl.semaphore_signal(barrier, inc=1, device_id=to_p, device_id_type=MESH)
    pl.semaphore_signal(barrier, inc=1, device_id=to_y, device_id_type=MESH)
    for line in order[1:]:
        for yy in (y, y_other):
            pl.semaphore_signal(
                barrier, inc=1, device_id=(x, place(line, yy, core)), device_id_type=MESH
            )
    low = images // 2

    def region(group, line, yy, kk):
        return maps.at[pl.ds(group * images, images), pl.ds(1 + place(line, yy, kk) * rows, rows)]

    def copy(src, dst, send, recv, to):
        return pltpu.make_async_remote_copy(
            src_ref=src, dst_ref=dst, send_sem=send, recv_sem=recv,
            device_id=to, device_id_type=MESH,
        )

    maps[pl.ds(x * images, images), pl.ds(1 + space * rows, rows)] = act[...]
    zeros = jnp.zeros((maps.shape[0], 1, columns, channels), maps.dtype)
    maps[:, 0:1] = zeros
    maps[:, height + 1 : height + 2] = zeros
    acc[...] = jnp.zeros_like(acc)
    gbuf[0] = grad[...].reshape(gbuf.shape[1:])
    pl.semaphore_wait(barrier, 9)

    own = region(x, z, y, core)
    x_copy = [copy(region(x, line, y, core), region(x, line, y, core), sx.at[n], rx.at[n], to_x)
              for n, line in enumerate(order)]
    y_copy = [copy(region(x, line, y, core), region(x, line, y, core), sy.at[n], ry.at[n], to_y)
              for n, line in enumerate(order)]
    dy_copy, dx_copy, p_copy = [], [], []
    for n, line in enumerate(order):
        from_x = maps.at[pl.ds(x_other * images, low), pl.ds(1 + place(line, y, core) * rows, rows)]
        from_y = maps.at[pl.ds(x * images + low, images - low),
                         pl.ds(1 + place(line, y_other, core) * rows, rows)]
        dy_copy.append(copy(from_x, from_x, sdy.at[n], rdy.at[n], to_y))
        dx_copy.append(copy(from_y, from_y, sdx.at[n], rdx.at[n], to_x))
        pair = []
        for m, yy in enumerate((y, y_other)):
            whole = maps.at[:, pl.ds(1 + place(line, yy, core) * rows, rows)]
            pair.append(copy(whole, whole, sp.at[n, m], rp.at[n, m], to_p))
        p_copy.append(pair)
    z_copy = [copy(own, own, sz.at[line], rz.at[z], (x, place(line, y, core))) for line in order[1:]]
    z_wait = [copy(region(x, line, y, core), region(x, line, y, core), sz.at[line], rz.at[line],
                   (x, place(line, y, core))) for line in order[1:]]

    x_copy[0].start()
    y_copy[0].start()
    for one in z_copy:
        one.start()
    gx = copy(gbuf.at[0], gbuf.at[1], sg.at[0], rg.at[0], to_x)
    gp0 = copy(gbuf.at[0], gbuf.at[2], sg.at[1], rg.at[1], to_p)
    gp1 = copy(gbuf.at[1], gbuf.at[3], sg.at[2], rg.at[2], to_p)
    gp0.start()
    gx.start()

    def forward_first(n):
        x_copy[n].wait_recv()
        dy_copy[n].start()
        y_copy[n].wait_recv()
        dx_copy[n].start()
        p_copy[n][0].start()

    def forward_second(n):
        dy_copy[n].wait_recv()
        dx_copy[n].wait_recv()
        p_copy[n][1].start()

    def forward_line(n):
        z_wait[n - 1].wait_recv()
        x_copy[n].start()
        y_copy[n].start()

    def wait_partner(n):
        p_copy[n][0].wait_recv()
        p_copy[n][1].wait_recv()

    forward_first(0)
    forward_line(1)
    gx.wait_recv()
    gp1.start()
    forward_line(2)
    forward_first(1)
    forward_second(0)
    forward_line(3)

    gp0.wait_recv()
    gp1.wait_recv()
    flat = gbuf[...].reshape(-1, channels)
    product = lax.dot_general(
        flat, flat, (((0,), (0,)), ((), ())), preferred_element_type=jnp.float32
    )
    gpart[...] = product.reshape(gpart.shape)
    grad_copies = []
    for n, line in enumerate(order):
        for m, yy in enumerate((y, y_other)):
            if n == 0 and m == 0:
                continue
            index = 2 * n + m
            one = copy(gpart.at[place(line, yy, core)], grecv.at[2 * z + y],
                       ss.at[index], rs.at[2 * z + y], (x, place(line, yy, core)))
            one.start()
            got = copy(gpart.at[place(line, yy, core)], grecv.at[2 * line + yy],
                       ss.at[index], rs.at[2 * line + yy], (x, place(line, yy, core)))
            grad_copies.append((one, got))

    me = x * spaces + space
    first = me * share
    tap_first = first // channels
    r = lax.broadcasted_iota(jnp.int32, (share, channels), 0) + first % channels
    c = lax.broadcasted_iota(jnp.int32, (share, channels), 1)
    select = [
        jnp.where(r == c, 1.0, 0.0).astype(maps.dtype),
        jnp.where(r == c + channels, 1.0, 0.0).astype(maps.dtype),
    ]
    taps = [tap_first, jnp.minimum(tap_first + 1, TAPS * TAPS - 1)]
    depth = 4 * rows
    width = depth * columns
    j = lax.broadcasted_iota(jnp.int32, (share, width), 1) % columns
    blocks = maps.shape[0]

    def right_of(image, row):
        return maps[image, pl.ds(row, depth)].reshape(width, channels)

    def chunk(image, line):
        start = 1 + line * depth
        left = None
        for u in range(2):
            dy, dx = taps[u] // TAPS - 1, taps[u] % TAPS - 1
            z_u = lax.dot_general(
                select[u], right_of(image, start + dy), (((1,), (1,)), ((), ())),
                preferred_element_type=jnp.float32,
            )
            z_u = pltpu.roll(z_u, (width - dx) % width, 1)
            z_u = jnp.where((j + dx >= 0) & (j + dx < columns), z_u, 0.0)
            left = z_u if left is None else left + z_u
        low_shift = jnp.where(j < columns - 1, pltpu.roll(left, width - 1, 1), 0.0)
        high_shift = jnp.where(j > 0, pltpu.roll(left, 1, 1), 0.0)
        stacked = jnp.concatenate([low_shift, left, high_shift], axis=0).astype(maps.dtype)
        for ky in range(TAPS):
            acc[ky] += jnp.dot(
                stacked, right_of(image, start + ky - 1), preferred_element_type=jnp.float32
            )

    def chunks(line_a, line_b):
        def body(step, carry):
            line = jnp.where(step < blocks, line_a, line_b)
            chunk(step % blocks, line)
            return carry

        lax.fori_loop(0, 2 * blocks, body, 0)

    forward_first(2)
    forward_second(1)
    wait_partner(0)
    wait_partner(1)
    forward_first(3)
    forward_second(2)
    wait_partner(2)
    forward_second(3)
    chunks(3 * half, 1 + half)
    wait_partner(3)
    chunks(3 - 3 * half, 2 - half)

    for ky in range(TAPS):
        for kx in range(TAPS):
            at = (TAPS * ky + kx) * channels
            sums[:, at : at + channels] = acc[ky, kx * share : (kx + 1) * share, :]
    total = gpart[space]
    for one, got in grad_copies:
        got.wait_recv()
    for n, line in enumerate(order):
        for m, yy in enumerate((y, y_other)):
            if n == 0 and m == 0:
                continue
            total = total + grecv[2 * line + yy]
    grad_sum[...] = total

    for one, got in grad_copies:
        one.wait_send()
    for one in x_copy + y_copy + dx_copy + dy_copy + z_copy + [gx, gp0, gp1]:
        one.wait_send()
    for pair in p_copy:
        pair[0].wait_send()
        pair[1].wait_send()


def kernel_form(activations, out_grads, old_input_factor, old_grad_factor):
    images, rows, columns, channels = activations.shape
    groups = lax.axis_size("dp")
    spaces = lax.axis_size("space")
    lines = spaces // 4
    height = rows * spaces
    positions = images * groups * height * columns
    share, width_all = old_input_factor.shape
    grad_share = old_grad_factor.shape[0]
    dma = pltpu.SemaphoreType.DMA
    vmem = pl.BlockSpec(memory_space=pltpu.VMEM)
    here = images * rows * columns
    input_sum, grad_sum = pl.pallas_call(
        gather_kernel,
        out_shape=(
            jax.ShapeDtypeStruct((share, width_all), jnp.float32),
            jax.ShapeDtypeStruct((grad_share, channels), jnp.float32),
        ),
        in_specs=[vmem, vmem],
        out_specs=(vmem, vmem),
        scratch_shapes=[
            pltpu.VMEM((images * groups, height + 2, columns, channels), activations.dtype),
            pltpu.VMEM((TAPS, TAPS * share, channels), jnp.float32),
            pltpu.VMEM((4, here, channels), out_grads.dtype),
            pltpu.VMEM((spaces, grad_share, channels), jnp.float32),
            pltpu.VMEM((2 * lines, grad_share, channels), jnp.float32),
        ]
        + [dma((lines,))] * 10
        + [dma((lines, 2))] * 2
        + [dma((3,))] * 2
        + [dma((2 * lines,))] * 2,
        compiler_params=pltpu.CompilerParams(
            collective_id=0, has_side_effects=True, vmem_limit_bytes=24 * 2**20
        ),
        cost_estimate=pl.CostEstimate(
            flops=2 * positions * share * width_all, bytes_accessed=4 * share * width_all,
            transcendentals=0,
        ),
    )(activations, out_grads)
    input_factor = 0.5 * old_input_factor.astype(jnp.float32) + 0.5 / positions * input_sum
    grad_factor = 0.5 * old_grad_factor + 0.5 / positions * grad_sum
    return input_factor, grad_factor


def per_device(activations, out_grads, old_input_factor, old_grad_factor):
    groups, spaces = lax.axis_size("dp"), lax.axis_size("space")
    images, channels = activations.shape[0], activations.shape[3]
    whole_map = activations.size * groups * spaces
    small = whole_map <= old_input_factor.shape[1] ** 2
    fits = groups == 2 and spaces == 16 and images % 2 == 0 and old_input_factor.shape[0] <= channels
    form = kernel_form if small and fits else reduced_form
    return form(activations, out_grads, old_input_factor, old_grad_factor)


def solution(mesh):
    return jax.shard_map(
        per_device,
        mesh=mesh,
        in_specs=(
            P("dp", "space", None, None),
            P("dp", "space", None, None),
            P(("dp", "space"), None),
            P("space", None),
        ),
        out_specs=(P(("dp", "space"), None), P("space", None)),
        check_vma=False,
    )
```

```python
import jax
import jax.numpy as jnp
from jax import lax
from jax.experimental import pallas as pl
from jax.experimental.pallas import tpu as pltpu
from jax.sharding import PartitionSpec as P


def extended(block, sides, width):
    for axis, dim in sides:
        count = lax.axis_size(axis)
        forward = [(i, i + 1) for i in range(count - 1)]
        backward = [(target, source) for source, target in forward]
        low = lax.ppermute(
            lax.slice_in_dim(block, block.shape[dim] - width, None, axis=dim), axis, forward
        )
        high = lax.ppermute(lax.slice_in_dim(block, 0, width, axis=dim), axis, backward)
        block = jnp.concatenate([low, block, high], axis=dim)
    return block


def transposed_product(left, right):
    return lax.dot_general(
        left, right, (((0,), (0,)), ((), ())), preferred_element_type=jnp.float32
    )


def reduced_form(activations, out_grads, old_input_factor, old_grad_factor):
    images, rows_here, columns_here, channels = activations.shape
    widened = extended(activations, (("space", 1),), 1)
    padded = jnp.pad(widened, ((0, 0), (0, 0), (1, 1), (0, 0)))
    pieces = [
        padded[:, ky : ky + rows_here, kx : kx + columns_here, :]
        for ky in range(3)
        for kx in range(3)
    ]
    patches = jnp.concatenate(pieces, axis=3).reshape(
        images * rows_here * columns_here, 9 * channels
    )
    groups = lax.axis_size("dp")
    spaces = lax.axis_size("space")
    positions = images * groups * rows_here * spaces * columns_here
    share = old_input_factor.shape[0]
    width_all = patches.shape[1]
    column_blocks = 4
    block_width = width_all // column_blocks
    results = []
    block = share * groups
    for which in range(column_blocks):
        right = patches[:, which * block_width : (which + 1) * block_width]

        def mapped_block(start, count, right=right):
            offsets = jnp.arange(count, dtype=jnp.int32)
            holder_space = offsets // block
            within_block = offsets % block
            holder_group = within_block // share
            within = within_block % share
            columns = holder_group * (spaces * share) + holder_space * share + within
            left = jnp.take(patches, columns, axis=1)
            return transposed_product(left, right)

        results.append(
            lax.psum_scatter(
                mapped_block(jnp.int32(0), block * lax.axis_size("space")),
                "space",
                scatter_dimension=0,
                tiled=True,
            )
        )
    part_sum = jnp.concatenate(results, axis=1)
    input_sum = lax.psum_scatter(
        part_sum.astype(jnp.bfloat16), "dp", scatter_dimension=0, tiled=True
    ).astype(jnp.float32)
    flat_grads = out_grads.reshape(images * rows_here * columns_here, channels)
    grad_term = transposed_product(flat_grads, flat_grads)
    grad_rows_here = old_grad_factor.shape[0]
    grad_total = lax.psum(grad_term, ("dp", "space"))
    grad_sum = lax.dynamic_slice_in_dim(
        grad_total, lax.axis_index("space") * grad_rows_here, grad_rows_here, 0
    )
    input_factor = 0.5 * old_input_factor.astype(jnp.float32) + 0.5 / positions * input_sum
    grad_factor = 0.5 * old_grad_factor + 0.5 / positions * grad_sum
    return (input_factor, grad_factor)


MESH = pl.DeviceIdType.MESH
TAPS = 3


def gather_kernel(act, grad, sums, grad_sum, maps, gbuf, gpart, grecv, here_sem,
                  sz, rz, sx, rx, sy, ry, sdx, rdx, sdy, rdy, sp, rp, sg, rg, ss, rs):
    images, rows, columns, channels = act.shape
    share = sums.shape[0]
    height = maps.shape[1] - 2
    spaces = height // rows
    lines = spaces // 4
    x = lax.axis_index("dp")
    space = lax.axis_index("space")
    core = space % 2
    y = (space // 2) % 2
    z = space // 4
    half = z // 2
    order = [z, z + 1 - 2 * (z % 2), 2 - half, 3 - 3 * half]
    x_other, y_other = 1 - x, 1 - y

    def place(line, yy, kk):
        return line * 4 + yy * 2 + kk

    to_x = (x_other, space)
    to_y = (x, place(z, y_other, core))
    to_p = (x, place(z, y, 1 - core))
    to_grad = [(line, flip) for flip in range(2) for line in range(lines)]

    barrier = pltpu.get_barrier_semaphore()
    pl.semaphore_signal(barrier, inc=1, device_id=to_x, device_id_type=MESH)
    pl.semaphore_signal(barrier, inc=1, device_id=to_p, device_id_type=MESH)
    pl.semaphore_signal(barrier, inc=1, device_id=to_y, device_id_type=MESH)
    for line in order[1:]:
        for yy in (y, y_other):
            pl.semaphore_signal(
                barrier, inc=1, device_id=(x, place(line, yy, core)), device_id_type=MESH
            )
    low = images // 2

    def region(group, line, yy, kk):
        return maps.at[pl.ds(group * images, images), pl.ds(1 + place(line, yy, kk) * rows, rows)]

    def copy(src, dst, send, recv, to):
        return pltpu.make_async_remote_copy(
            src_ref=src, dst_ref=dst, send_sem=send, recv_sem=recv,
            device_id=to, device_id_type=MESH,
        )

    own = region(x, z, y, core)
    keep = pltpu.make_async_copy(act, own, here_sem.at[0])
    keep_grad = pltpu.make_async_copy(grad, gbuf.at[0], here_sem.at[1])
    keep.start()
    keep_grad.start()
    zeros = jnp.zeros((maps.shape[0], 1, columns, channels), maps.dtype)
    maps[:, 0:1] = zeros
    maps[:, height + 1 : height + 2] = zeros
    pl.semaphore_wait(barrier, 9)

    x_copy = [copy(region(x, line, y, core) if n else act, region(x, line, y, core), sx.at[n], rx.at[n], to_x)
              for n, line in enumerate(order)]
    y_copy = [copy(region(x, line, y, core) if n else act, region(x, line, y, core), sy.at[n], ry.at[n], to_y)
              for n, line in enumerate(order)]
    dy_copy, dx_copy, p_copy = [], [], []
    for n, line in enumerate(order):
        from_x = maps.at[pl.ds(x_other * images, low), pl.ds(1 + place(line, y, core) * rows, rows)]
        from_y = maps.at[pl.ds(x * images + low, images - low),
                         pl.ds(1 + place(line, y_other, core) * rows, rows)]
        dy_copy.append(copy(from_x, from_x, sdy.at[n], rdy.at[n], to_y))
        dx_copy.append(copy(from_y, from_y, sdx.at[n], rdx.at[n], to_x))
        pair = []
        for m, yy in enumerate((y, y_other)):
            whole = maps.at[:, pl.ds(1 + place(line, yy, core) * rows, rows)]
            pair.append(copy(whole, whole, sp.at[n, m], rp.at[n, m], to_p))
        p_copy.append(pair)
    z_copy = [copy(act, own, sz.at[line], rz.at[z], (x, place(line, y, core))) for line in order[1:]]
    z_wait = [copy(region(x, line, y, core), region(x, line, y, core), sz.at[line], rz.at[line],
                   (x, place(line, y, core))) for line in order[1:]]

    x_copy[0].start()
    y_copy[0].start()
    for one in z_copy:
        one.start()
    gx = copy(grad, gbuf.at[1], sg.at[0], rg.at[0], to_x)
    gp0 = copy(grad, gbuf.at[2], sg.at[1], rg.at[1], to_p)
    gp1 = copy(gbuf.at[1], gbuf.at[3], sg.at[2], rg.at[2], to_p)
    gp0.start()
    gx.start()

    def forward_first(n):
        x_copy[n].wait_recv()
        dy_copy[n].start()
        y_copy[n].wait_recv()
        dx_copy[n].start()
        p_copy[n][0].start()

    def forward_second(n):
        dy_copy[n].wait_recv()
        dx_copy[n].wait_recv()
        p_copy[n][1].start()

    def forward_line(n):
        z_wait[n - 1].wait_recv()
        x_copy[n].start()
        y_copy[n].start()

    def wait_partner(n):
        p_copy[n][0].wait_recv()
        p_copy[n][1].wait_recv()

    keep.wait()
    forward_first(0)
    forward_line(1)
    gx.wait_recv()
    gp1.start()
    forward_line(2)
    forward_second(0)
    forward_first(1)
    forward_line(3)

    keep_grad.wait()
    gp0.wait_recv()
    gp1.wait_recv()
    flat = gbuf[...].reshape(-1, channels)
    product = lax.dot_general(
        flat, flat, (((0,), (0,)), ((), ())), preferred_element_type=jnp.float32
    )
    gpart[...] = product.reshape(gpart.shape)
    grad_copies = []
    for n, line in enumerate(order):
        for m, yy in enumerate((y, y_other)):
            if n == 0 and m == 0:
                continue
            index = 2 * n + m
            one = copy(gpart.at[place(line, yy, core)], grecv.at[2 * z + y],
                       ss.at[index], rs.at[2 * z + y], (x, place(line, yy, core)))
            one.start()
            got = copy(gpart.at[place(line, yy, core)], grecv.at[2 * line + yy],
                       ss.at[index], rs.at[2 * line + yy], (x, place(line, yy, core)))
            grad_copies.append((one, got))

    me = x * spaces + space
    first = me * share
    tap_first = first // channels
    r = lax.broadcasted_iota(jnp.int32, (share, channels), 0) + first % channels
    c = lax.broadcasted_iota(jnp.int32, (share, channels), 1)
    select = jnp.concatenate(
        [jnp.where(r == c, 1.0, 0.0), jnp.where(r == c + channels, 1.0, 0.0)], axis=1
    ).astype(maps.dtype)
    tap_next = jnp.minimum(tap_first + 1, TAPS * TAPS - 1)
    edge = channels - first % channels
    blocks = maps.shape[0]

    def stage(start, depth):
        width = blocks * depth * columns
        row = lax.broadcasted_iota(jnp.int32, (share, width), 0)
        j = lax.broadcasted_iota(jnp.int32, (share, width), 1) % columns
        shift = jnp.where(row < edge, tap_first % TAPS, tap_next % TAPS) - 1

        def right_of(move):
            return maps[:, pl.ds(1 + start + move, depth)].reshape(width, channels)

        both = jnp.concatenate(
            [right_of(tap_first // TAPS - 1), right_of(tap_next // TAPS - 1)], axis=1
        )
        picked = lax.dot_general(
            select, both, (((1,), (1,)), ((), ())), preferred_element_type=jnp.float32
        )

        def lower(value):
            return jnp.where(j < columns - 1, pltpu.roll(value, width - 1, 1), 0.0)

        def higher(value):
            return jnp.where(j > 0, pltpu.roll(value, 1, 1), 0.0)

        left = jnp.where(
            shift == 0, picked, jnp.where(shift > 0, lower(picked), higher(picked))
        )
        stacked = jnp.concatenate([lower(left), left, higher(left)], axis=0).astype(maps.dtype)
        for ky in range(TAPS):
            part = jnp.dot(stacked, right_of(ky - 1), preferred_element_type=jnp.float32)
            for kx in range(TAPS):
                at = (TAPS * ky + kx) * channels
                piece = part[kx * share : (kx + 1) * share]
                if fresh[0]:
                    sums[:, at : at + channels] = piece
                else:
                    sums[:, at : at + channels] += piece
        fresh[0] = False

    fresh = [True]
    line_rows = 4 * rows
    side = line_rows + line_rows // 2
    forward_first(2)
    forward_second(1)
    wait_partner(0)
    wait_partner(1)
    stage(half * (height - side), side)
    forward_first(3)
    forward_second(2)
    wait_partner(2)
    stage(side, height - 2 * side)
    forward_second(3)
    wait_partner(3)
    stage((1 - half) * (height - side), side)

    total = gpart[space]
    for one, got in grad_copies:
        got.wait_recv()
    for n, line in enumerate(order):
        for m, yy in enumerate((y, y_other)):
            if n == 0 and m == 0:
                continue
            total = total + grecv[2 * line + yy]
    grad_sum[...] = total

    for one, got in grad_copies:
        one.wait_send()
    for one in x_copy + y_copy + dx_copy + dy_copy + z_copy + [gx, gp0, gp1]:
        one.wait_send()
    for pair in p_copy:
        pair[0].wait_send()
        pair[1].wait_send()


def kernel_form(activations, out_grads, old_input_factor, old_grad_factor):
    images, rows, columns, channels = activations.shape
    groups = lax.axis_size("dp")
    spaces = lax.axis_size("space")
    lines = spaces // 4
    height = rows * spaces
    positions = images * groups * height * columns
    share, width_all = old_input_factor.shape
    grad_share = old_grad_factor.shape[0]
    dma = pltpu.SemaphoreType.DMA
    vmem = pl.BlockSpec(memory_space=pltpu.VMEM)
    hbm = pl.BlockSpec(memory_space=pltpu.HBM)
    input_sum, grad_sum = pl.pallas_call(
        gather_kernel,
        out_shape=(
            jax.ShapeDtypeStruct((share, width_all), jnp.float32),
            jax.ShapeDtypeStruct((grad_share, channels), jnp.float32),
        ),
        in_specs=[hbm, hbm],
        out_specs=(vmem, vmem),
        scratch_shapes=[
            pltpu.VMEM((images * groups, height + 2, columns, channels), activations.dtype),
            pltpu.VMEM((4,) + out_grads.shape, out_grads.dtype),
            pltpu.VMEM((spaces, grad_share, channels), jnp.float32),
            pltpu.VMEM((2 * lines, grad_share, channels), jnp.float32),
        ]
        + [dma((2,))]
        + [dma((lines,))] * 10
        + [dma((lines, 2))] * 2
        + [dma((3,))] * 2
        + [dma((2 * lines,))] * 2,
        compiler_params=pltpu.CompilerParams(
            collective_id=0, has_side_effects=True, vmem_limit_bytes=24 * 2**20
        ),
        cost_estimate=pl.CostEstimate(
            flops=2 * positions * share * width_all, bytes_accessed=4 * share * width_all,
            transcendentals=0,
        ),
    )(activations, out_grads)
    input_factor = 0.5 * old_input_factor.astype(jnp.float32) + 0.5 / positions * input_sum
    grad_factor = 0.5 * old_grad_factor + 0.5 / positions * grad_sum
    return input_factor, grad_factor


def per_device(activations, out_grads, old_input_factor, old_grad_factor):
    groups, spaces = lax.axis_size("dp"), lax.axis_size("space")
    images, channels = activations.shape[0], activations.shape[3]
    whole_map = activations.size * groups * spaces
    small = whole_map <= old_input_factor.shape[1] ** 2
    fits = groups == 2 and spaces == 16 and images % 2 == 0 and old_input_factor.shape[0] <= channels
    form = kernel_form if small and fits else reduced_form
    return form(activations, out_grads, old_input_factor, old_grad_factor)


def solution(mesh):
    return jax.shard_map(
        per_device,
        mesh=mesh,
        in_specs=(
            P("dp", "space", None, None),
            P("dp", "space", None, None),
            P(("dp", "space"), None),
            P("space", None),
        ),
        out_specs=(P(("dp", "space"), None), P("space", None)),
        check_vma=False,
    )
```

```python
import jax
import jax.numpy as jnp
from jax import lax
from jax.experimental import pallas as pl
from jax.experimental.pallas import tpu as pltpu
from jax.sharding import PartitionSpec as P


def extended(block, sides, width):
    for axis, dim in sides:
        count = lax.axis_size(axis)
        forward = [(i, i + 1) for i in range(count - 1)]
        backward = [(target, source) for source, target in forward]
        low = lax.ppermute(
            lax.slice_in_dim(block, block.shape[dim] - width, None, axis=dim), axis, forward
        )
        high = lax.ppermute(lax.slice_in_dim(block, 0, width, axis=dim), axis, backward)
        block = jnp.concatenate([low, block, high], axis=dim)
    return block


def transposed_product(left, right):
    return lax.dot_general(
        left, right, (((0,), (0,)), ((), ())), preferred_element_type=jnp.float32
    )


def reduced_form(activations, out_grads, old_input_factor, old_grad_factor):
    images, rows_here, columns_here, channels = activations.shape
    widened = extended(activations, (("space", 1),), 1)
    padded = jnp.pad(widened, ((0, 0), (0, 0), (1, 1), (0, 0)))
    pieces = [
        padded[:, ky : ky + rows_here, kx : kx + columns_here, :]
        for ky in range(3)
        for kx in range(3)
    ]
    patches = jnp.concatenate(pieces, axis=3).reshape(
        images * rows_here * columns_here, 9 * channels
    )
    groups = lax.axis_size("dp")
    spaces = lax.axis_size("space")
    positions = images * groups * rows_here * spaces * columns_here
    share = old_input_factor.shape[0]
    width_all = patches.shape[1]
    column_blocks = 4
    block_width = width_all // column_blocks
    results = []
    block = share * groups
    for which in range(column_blocks):
        right = patches[:, which * block_width : (which + 1) * block_width]

        def mapped_block(start, count, right=right):
            offsets = jnp.arange(count, dtype=jnp.int32)
            holder_space = offsets // block
            within_block = offsets % block
            holder_group = within_block // share
            within = within_block % share
            columns = holder_group * (spaces * share) + holder_space * share + within
            left = jnp.take(patches, columns, axis=1)
            return transposed_product(left, right)

        results.append(
            lax.psum_scatter(
                mapped_block(jnp.int32(0), block * lax.axis_size("space")),
                "space",
                scatter_dimension=0,
                tiled=True,
            )
        )
    part_sum = jnp.concatenate(results, axis=1)
    input_sum = lax.psum_scatter(
        part_sum.astype(jnp.bfloat16), "dp", scatter_dimension=0, tiled=True
    ).astype(jnp.float32)
    flat_grads = out_grads.reshape(images * rows_here * columns_here, channels)
    grad_term = transposed_product(flat_grads, flat_grads)
    grad_rows_here = old_grad_factor.shape[0]
    grad_total = lax.psum(grad_term, ("dp", "space"))
    grad_sum = lax.dynamic_slice_in_dim(
        grad_total, lax.axis_index("space") * grad_rows_here, grad_rows_here, 0
    )
    input_factor = 0.5 * old_input_factor.astype(jnp.float32) + 0.5 / positions * input_sum
    grad_factor = 0.5 * old_grad_factor + 0.5 / positions * grad_sum
    return (input_factor, grad_factor)


MESH = pl.DeviceIdType.MESH
TAPS = 3


def gather_kernel(act, grad, sums, grad_sum, maps, gbuf, gpart, grecv, here_sem,
                  sz, rz, sx, rx, sy, ry, sdx, rdx, sdy, rdy, sp, rp, sg, rg, ss, rs):
    images, rows, columns, channels = act.shape
    share = sums.shape[0]
    height = maps.shape[1] - 2
    spaces = height // rows
    lines = spaces // 4
    x = lax.axis_index("dp")
    space = lax.axis_index("space")
    core = space % 2
    y = (space // 2) % 2
    z = space // 4
    half = z // 2
    order = [z, z + 1 - 2 * (z % 2), 2 - half, 3 - 3 * half]
    x_other, y_other = 1 - x, 1 - y

    def place(line, yy, kk):
        return line * 4 + yy * 2 + kk

    to_x = (x_other, space)
    to_y = (x, place(z, y_other, core))
    to_p = (x, place(z, y, 1 - core))

    barrier = pltpu.get_barrier_semaphore()
    pl.semaphore_signal(barrier, inc=1, device_id=to_x, device_id_type=MESH)
    pl.semaphore_signal(barrier, inc=1, device_id=to_p, device_id_type=MESH)
    pl.semaphore_signal(barrier, inc=1, device_id=to_y, device_id_type=MESH)
    middle = (z % 3 + 1) // 2
    is_middle = middle == 1
    near = (x, place(jnp.where(is_middle, 3 * half, 1 + half), y, core))
    across = (x, place(3 - z, y, core))
    pl.semaphore_signal(barrier, inc=1, device_id=near, device_id_type=MESH)

    @pl.when(is_middle)
    def _():
        pl.semaphore_signal(barrier, inc=1, device_id=across, device_id_type=MESH)

    low = images // 2

    def region(group, line, yy, kk):
        return maps.at[pl.ds(group * images, images), pl.ds(1 + place(line, yy, kk) * rows, rows)]

    def copy(src, dst, send, recv, to):
        return pltpu.make_async_remote_copy(
            src_ref=src, dst_ref=dst, send_sem=send, recv_sem=recv,
            device_id=to, device_id_type=MESH,
        )

    own = region(x, z, y, core)
    keep = pltpu.make_async_copy(act, own, here_sem.at[0])
    keep_grad = pltpu.make_async_copy(grad, gbuf.at[0], here_sem.at[1])
    keep.start()
    keep_grad.start()
    zeros = jnp.zeros((maps.shape[0], 1, columns, channels), maps.dtype)
    maps[:, 0:1] = zeros
    maps[:, height + 1 : height + 2] = zeros
    pl.semaphore_wait(barrier, 4 + middle)

    x_copy = [copy(region(x, line, y, core) if n else act, region(x, line, y, core), sx.at[n], rx.at[n], to_x)
              for n, line in enumerate(order)]
    y_copy = [copy(region(x, line, y, core) if n else act, region(x, line, y, core), sy.at[n], ry.at[n], to_y)
              for n, line in enumerate(order)]
    dy_copy, dx_copy, p_copy = [], [], []
    for n, line in enumerate(order):
        from_x = maps.at[pl.ds(x_other * images, low), pl.ds(1 + place(line, y, core) * rows, rows)]
        from_y = maps.at[pl.ds(x * images + low, images - low),
                         pl.ds(1 + place(line, y_other, core) * rows, rows)]
        dy_copy.append(copy(from_x, from_x, sdy.at[n], rdy.at[n], to_y))
        dx_copy.append(copy(from_y, from_y, sdx.at[n], rdx.at[n], to_x))
        pair = []
        for m, yy in enumerate((y, y_other)):
            whole = maps.at[:, pl.ds(1 + place(line, yy, core) * rows, rows)]
            pair.append(copy(whole, whole, sp.at[n, m], rp.at[n, m], to_p))
        p_copy.append(pair)
    def z_block(n):
        return act if n == 0 else region(x, order[n], y, core)

    def z_send(n, to, slot):
        return copy(z_block(n), region(x, order[n], y, core), sz.at[slot], rz.at[order[n]], to)

    z_near = z_send(0, near, 0)
    z_across = z_send(0, across, 1)
    z_pass = {1: z_send(1, across, 2), 2: z_send(2, near, 3), 3: z_send(3, near, 4)}
    z_wait = [copy(region(x, line, y, core), region(x, line, y, core), sz.at[0], rz.at[line], near)
              for line in order[1:]]

    x_copy[0].start()
    y_copy[0].start()
    z_near.start()

    @pl.when(is_middle)
    def _():
        z_across.start()

    gx = copy(grad, gbuf.at[1], sg.at[0], rg.at[0], to_x)
    gp0 = copy(grad, gbuf.at[2], sg.at[1], rg.at[1], to_p)
    gp1 = copy(gbuf.at[1], gbuf.at[3], sg.at[2], rg.at[2], to_p)
    gp0.start()
    gx.start()

    def forward_first(n):
        x_copy[n].wait_recv()
        dy_copy[n].start()
        y_copy[n].wait_recv()
        dx_copy[n].start()
        p_copy[n][0].start()

    def forward_second(n):
        dy_copy[n].wait_recv()
        dx_copy[n].wait_recv()
        p_copy[n][1].start()

    def forward_line(n):
        z_wait[n - 1].wait_recv()

        @pl.when(is_middle)
        def _():
            z_pass[n].start()

        x_copy[n].start()
        y_copy[n].start()

    def wait_partner(n):
        p_copy[n][0].wait_recv()
        p_copy[n][1].wait_recv()

    keep.wait()
    forward_first(0)
    forward_line(1)
    gx.wait_recv()
    gp1.start()
    forward_line(2)
    forward_second(0)
    forward_first(1)
    forward_line(3)

    keep_grad.wait()
    gp0.wait_recv()
    gp1.wait_recv()
    flat = gbuf[...].reshape(-1, channels)
    product = lax.dot_general(
        flat, flat, (((0,), (0,)), ((), ())), preferred_element_type=jnp.float32
    )
    gpart[...] = product.reshape(gpart.shape)
    me = x * spaces + space
    first = me * share
    tap_first = first // channels
    r = lax.broadcasted_iota(jnp.int32, (share, channels), 0) + first % channels
    c = lax.broadcasted_iota(jnp.int32, (share, channels), 1)
    select = jnp.concatenate(
        [jnp.where(r == c, 1.0, 0.0), jnp.where(r == c + channels, 1.0, 0.0)], axis=1
    ).astype(maps.dtype)
    tap_next = jnp.minimum(tap_first + 1, TAPS * TAPS - 1)
    edge = channels - first % channels
    blocks = maps.shape[0]

    def stage(start, depth):
        width = blocks * depth * columns
        row = lax.broadcasted_iota(jnp.int32, (share, width), 0)
        j = lax.broadcasted_iota(jnp.int32, (share, width), 1) % columns
        shift = jnp.where(row < edge, tap_first % TAPS, tap_next % TAPS) - 1

        def right_of(move):
            return maps[:, pl.ds(1 + start + move, depth)].reshape(width, channels)

        both = jnp.concatenate(
            [right_of(tap_first // TAPS - 1), right_of(tap_next // TAPS - 1)], axis=1
        )
        picked = lax.dot_general(
            select, both, (((1,), (1,)), ((), ())), preferred_element_type=jnp.float32
        )

        def lower(value):
            return jnp.where(j < columns - 1, pltpu.roll(value, width - 1, 1), 0.0)

        def higher(value):
            return jnp.where(j > 0, pltpu.roll(value, 1, 1), 0.0)

        left = jnp.where(
            shift == 0, picked, jnp.where(shift > 0, lower(picked), higher(picked))
        )
        stacked = jnp.concatenate([lower(left), left, higher(left)], axis=0).astype(maps.dtype)
        for ky in range(TAPS):
            part = jnp.dot(stacked, right_of(ky - 1), preferred_element_type=jnp.float32)
            for kx in range(TAPS):
                at = (TAPS * ky + kx) * channels
                piece = part[kx * share : (kx + 1) * share]
                if fresh[0]:
                    sums[:, at : at + channels] = piece
                else:
                    sums[:, at : at + channels] += piece
        fresh[0] = False

    fresh = [True]
    line_rows = 4 * rows
    side = line_rows + line_rows // 2
    forward_first(2)
    forward_second(1)
    wait_partner(0)
    wait_partner(1)
    stage(half * (height - side), side)
    forward_first(3)
    grad_copies = []
    for n, line in enumerate(order):
        for m, yy in enumerate((y, y_other)):
            if n == 0 and m == 0:
                continue
            index = 2 * n + m
            one = copy(gpart.at[place(line, yy, core)], grecv.at[2 * z + y],
                       ss.at[index], rs.at[2 * z + y], (x, place(line, yy, core)))
            one.start()
            got = copy(gpart.at[place(line, yy, core)], grecv.at[2 * line + yy],
                       ss.at[index], rs.at[2 * line + yy], (x, place(line, yy, core)))
            grad_copies.append((one, got))

    forward_second(2)
    wait_partner(2)
    stage(side, height - 2 * side)
    forward_second(3)
    wait_partner(3)
    stage((1 - half) * (height - side), side)

    total = gpart[space]
    for one, got in grad_copies:
        got.wait_recv()
    for n, line in enumerate(order):
        for m, yy in enumerate((y, y_other)):
            if n == 0 and m == 0:
                continue
            total = total + grecv[2 * line + yy]
    grad_sum[...] = total

    for one, got in grad_copies:
        one.wait_send()
    for one in x_copy + y_copy + dx_copy + dy_copy + [z_near, gx, gp0, gp1]:
        one.wait_send()

    @pl.when(is_middle)
    def _():
        z_across.wait_send()
        for n in z_pass:
            z_pass[n].wait_send()

    for pair in p_copy:
        pair[0].wait_send()
        pair[1].wait_send()


def kernel_form(activations, out_grads, old_input_factor, old_grad_factor):
    images, rows, columns, channels = activations.shape
    groups = lax.axis_size("dp")
    spaces = lax.axis_size("space")
    lines = spaces // 4
    height = rows * spaces
    positions = images * groups * height * columns
    share, width_all = old_input_factor.shape
    grad_share = old_grad_factor.shape[0]
    dma = pltpu.SemaphoreType.DMA
    vmem = pl.BlockSpec(memory_space=pltpu.VMEM)
    hbm = pl.BlockSpec(memory_space=pltpu.HBM)
    input_sum, grad_sum = pl.pallas_call(
        gather_kernel,
        out_shape=(
            jax.ShapeDtypeStruct((share, width_all), jnp.float32),
            jax.ShapeDtypeStruct((grad_share, channels), jnp.float32),
        ),
        in_specs=[hbm, hbm],
        out_specs=(vmem, vmem),
        scratch_shapes=[
            pltpu.VMEM((images * groups, height + 2, columns, channels), activations.dtype),
            pltpu.VMEM((4,) + out_grads.shape, out_grads.dtype),
            pltpu.VMEM((spaces, grad_share, channels), jnp.float32),
            pltpu.VMEM((2 * lines, grad_share, channels), jnp.float32),
        ]
        + [dma((2,))]
        + [dma((lines + 1,)), dma((lines,))]
        + [dma((lines,))] * 8
        + [dma((lines, 2))] * 2
        + [dma((3,))] * 2
        + [dma((2 * lines,))] * 2,
        compiler_params=pltpu.CompilerParams(
            collective_id=0, has_side_effects=True, vmem_limit_bytes=24 * 2**20
        ),
        cost_estimate=pl.CostEstimate(
            flops=2 * positions * share * width_all, bytes_accessed=4 * share * width_all,
            transcendentals=0,
        ),
    )(activations, out_grads)
    input_factor = 0.5 * old_input_factor.astype(jnp.float32) + 0.5 / positions * input_sum
    grad_factor = 0.5 * old_grad_factor + 0.5 / positions * grad_sum
    return input_factor, grad_factor


def per_device(activations, out_grads, old_input_factor, old_grad_factor):
    groups, spaces = lax.axis_size("dp"), lax.axis_size("space")
    images, channels = activations.shape[0], activations.shape[3]
    whole_map = activations.size * groups * spaces
    small = whole_map <= old_input_factor.shape[1] ** 2
    fits = groups == 2 and spaces == 16 and images % 2 == 0 and old_input_factor.shape[0] <= channels
    form = kernel_form if small and fits else reduced_form
    return form(activations, out_grads, old_input_factor, old_grad_factor)


def solution(mesh):
    return jax.shard_map(
        per_device,
        mesh=mesh,
        in_specs=(
            P("dp", "space", None, None),
            P("dp", "space", None, None),
            P(("dp", "space"), None),
            P("space", None),
        ),
        out_specs=(P(("dp", "space"), None), P("space", None)),
        check_vma=False,
    )
```

```python
import jax
import jax.numpy as jnp
from jax import lax
from jax.experimental import pallas as pl
from jax.experimental.pallas import tpu as pltpu
from jax.sharding import PartitionSpec as P


def extended(block, sides, width):
    for axis, dim in sides:
        count = lax.axis_size(axis)
        forward = [(i, i + 1) for i in range(count - 1)]
        backward = [(target, source) for source, target in forward]
        low = lax.ppermute(
            lax.slice_in_dim(block, block.shape[dim] - width, None, axis=dim), axis, forward
        )
        high = lax.ppermute(lax.slice_in_dim(block, 0, width, axis=dim), axis, backward)
        block = jnp.concatenate([low, block, high], axis=dim)
    return block


def transposed_product(left, right):
    return lax.dot_general(
        left, right, (((0,), (0,)), ((), ())), preferred_element_type=jnp.float32
    )


def reduced_form(activations, out_grads, old_input_factor, old_grad_factor):
    images, rows_here, columns_here, channels = activations.shape
    widened = extended(activations, (("space", 1),), 1)
    padded = jnp.pad(widened, ((0, 0), (0, 0), (1, 1), (0, 0)))
    pieces = [
        padded[:, ky : ky + rows_here, kx : kx + columns_here, :]
        for ky in range(3)
        for kx in range(3)
    ]
    patches = jnp.concatenate(pieces, axis=3).reshape(
        images * rows_here * columns_here, 9 * channels
    )
    groups = lax.axis_size("dp")
    spaces = lax.axis_size("space")
    positions = images * groups * rows_here * spaces * columns_here
    share = old_input_factor.shape[0]
    width_all = patches.shape[1]
    column_blocks = 4
    block_width = width_all // column_blocks
    results = []
    block = share * groups
    for which in range(column_blocks):
        right = patches[:, which * block_width : (which + 1) * block_width]

        def mapped_block(start, count, right=right):
            offsets = jnp.arange(count, dtype=jnp.int32)
            holder_space = offsets // block
            within_block = offsets % block
            holder_group = within_block // share
            within = within_block % share
            columns = holder_group * (spaces * share) + holder_space * share + within
            left = jnp.take(patches, columns, axis=1)
            return transposed_product(left, right)

        results.append(
            lax.psum_scatter(
                mapped_block(jnp.int32(0), block * lax.axis_size("space")),
                "space",
                scatter_dimension=0,
                tiled=True,
            )
        )
    part_sum = jnp.concatenate(results, axis=1)
    input_sum = lax.psum_scatter(
        part_sum.astype(jnp.bfloat16), "dp", scatter_dimension=0, tiled=True
    ).astype(jnp.float32)
    flat_grads = out_grads.reshape(images * rows_here * columns_here, channels)
    grad_term = transposed_product(flat_grads, flat_grads)
    grad_rows_here = old_grad_factor.shape[0]
    grad_total = lax.psum(grad_term, ("dp", "space"))
    grad_sum = lax.dynamic_slice_in_dim(
        grad_total, lax.axis_index("space") * grad_rows_here, grad_rows_here, 0
    )
    input_factor = 0.5 * old_input_factor.astype(jnp.float32) + 0.5 / positions * input_sum
    grad_factor = 0.5 * old_grad_factor + 0.5 / positions * grad_sum
    return (input_factor, grad_factor)


MESH = pl.DeviceIdType.MESH
TAPS = 3


def gather_kernel(act, grad, sums, grad_sum, maps, gbuf, gpart, grecv, here_sem,
                  sz, rz, sx, rx, sy, ry, sdx, rdx, sdy, rdy, sp, rp, sg, rg, ss, rs):
    images, rows, columns, channels = act.shape
    share = sums.shape[0]
    height = maps.shape[1] - 2
    spaces = height // rows
    lines = spaces // 4
    x = lax.axis_index("dp")
    space = lax.axis_index("space")
    core = space % 2
    y = (space // 2) % 2
    z = space // 4
    half = z // 2
    order = [z, z + 1 - 2 * (z % 2), 2 - half, 3 - 3 * half]
    x_other, y_other = 1 - x, 1 - y

    def place(line, yy, kk):
        return line * 4 + yy * 2 + kk

    to_x = (x_other, space)
    to_y = (x, place(z, y_other, core))
    to_p = (x, place(z, y, 1 - core))

    barrier = pltpu.get_barrier_semaphore()
    pl.semaphore_signal(barrier, inc=1, device_id=to_x, device_id_type=MESH)
    pl.semaphore_signal(barrier, inc=1, device_id=to_p, device_id_type=MESH)
    pl.semaphore_signal(barrier, inc=1, device_id=to_y, device_id_type=MESH)
    middle = (z % 3 + 1) // 2
    is_middle = middle == 1
    near = (x, place(jnp.where(is_middle, 3 * half, 1 + half), y, core))
    across = (x, place(3 - z, y, core))
    pl.semaphore_signal(barrier, inc=1, device_id=near, device_id_type=MESH)

    @pl.when(is_middle)
    def _():
        pl.semaphore_signal(barrier, inc=1, device_id=across, device_id_type=MESH)

    low = images // 2

    def region(group, line, yy, kk):
        return maps.at[pl.ds(group * images, images), pl.ds(1 + place(line, yy, kk) * rows, rows)]

    def copy(src, dst, send, recv, to):
        return pltpu.make_async_remote_copy(
            src_ref=src, dst_ref=dst, send_sem=send, recv_sem=recv,
            device_id=to, device_id_type=MESH,
        )

    own = region(x, z, y, core)
    keep = pltpu.make_async_copy(act, own, here_sem.at[0])
    keep_grad = pltpu.make_async_copy(grad, gbuf.at[0], here_sem.at[1])
    keep.start()
    keep_grad.start()
    zeros = jnp.zeros((maps.shape[0], 1, columns, channels), maps.dtype)
    maps[:, 0:1] = zeros
    maps[:, height + 1 : height + 2] = zeros
    pl.semaphore_wait(barrier, 4 + middle)

    x_copy = [copy(region(x, line, y, core) if n else act, region(x, line, y, core), sx.at[n], rx.at[n], to_x)
              for n, line in enumerate(order)]
    y_copy = [copy(region(x, line, y, core) if n else act, region(x, line, y, core), sy.at[n], ry.at[n], to_y)
              for n, line in enumerate(order)]
    dy_copy, dx_copy, p_copy = [], [], []
    for n, line in enumerate(order):
        from_x = maps.at[pl.ds(x_other * images, low), pl.ds(1 + place(line, y, core) * rows, rows)]
        from_y = maps.at[pl.ds(x * images + low, images - low),
                         pl.ds(1 + place(line, y_other, core) * rows, rows)]
        dy_copy.append(copy(from_x, from_x, sdy.at[n], rdy.at[n], to_y))
        dx_copy.append(copy(from_y, from_y, sdx.at[n], rdx.at[n], to_x))
        pair = []
        for m, yy in enumerate((y, y_other)):
            whole = maps.at[:, pl.ds(1 + place(line, yy, core) * rows, rows)]
            pair.append(copy(whole, whole, sp.at[n, m], rp.at[n, m], to_p))
        p_copy.append(pair)
    def z_block(n):
        return act if n == 0 else region(x, order[n], y, core)

    def z_send(n, to, slot):
        return copy(z_block(n), region(x, order[n], y, core), sz.at[slot], rz.at[order[n]], to)

    z_near = z_send(0, near, 0)
    z_across = z_send(0, across, 1)
    z_pass = {1: z_send(1, across, 2), 2: z_send(2, near, 3), 3: z_send(3, near, 4)}
    z_wait = [copy(region(x, line, y, core), region(x, line, y, core), sz.at[0], rz.at[line], near)
              for line in order[1:]]

    x_copy[0].start()
    y_copy[0].start()
    z_near.start()

    @pl.when(is_middle)
    def _():
        z_across.start()

    gx = copy(grad, gbuf.at[1], sg.at[0], rg.at[0], to_x)
    gp0 = copy(grad, gbuf.at[2], sg.at[1], rg.at[1], to_p)
    gp1 = copy(gbuf.at[1], gbuf.at[3], sg.at[2], rg.at[2], to_p)

    def forward_first(n):
        x_copy[n].wait_recv()
        dy_copy[n].start()
        y_copy[n].wait_recv()
        dx_copy[n].start()
        p_copy[n][0].start()

    def forward_second(n):
        dy_copy[n].wait_recv()
        dx_copy[n].wait_recv()
        p_copy[n][1].start()

    def forward_line(n):
        z_wait[n - 1].wait_recv()

        @pl.when(is_middle)
        def _():
            z_pass[n].start()

        x_copy[n].start()
        y_copy[n].start()

    def wait_partner(n):
        p_copy[n][0].wait_recv()
        p_copy[n][1].wait_recv()

    keep.wait()
    forward_line(1)
    forward_first(0)
    gp0.start()
    gx.start()
    forward_line(2)
    forward_line(3)
    forward_first(1)
    forward_second(0)
    gx.wait_recv()
    gp1.start()

    keep_grad.wait()
    gp0.wait_recv()
    gp1.wait_recv()
    flat = gbuf[...].reshape(-1, channels)
    product = lax.dot_general(
        flat, flat, (((0,), (0,)), ((), ())), preferred_element_type=jnp.float32
    )
    gpart[...] = product.reshape(gpart.shape)
    me = x * spaces + space
    first = me * share
    tap_first = first // channels
    r = lax.broadcasted_iota(jnp.int32, (share, channels), 0) + first % channels
    c = lax.broadcasted_iota(jnp.int32, (share, channels), 1)
    select = jnp.concatenate(
        [jnp.where(r == c, 1.0, 0.0), jnp.where(r == c + channels, 1.0, 0.0)], axis=1
    ).astype(maps.dtype)
    tap_next = jnp.minimum(tap_first + 1, TAPS * TAPS - 1)
    edge = channels - first % channels
    blocks = maps.shape[0]

    def stage(start, depth):
        width = blocks * depth * columns
        row = lax.broadcasted_iota(jnp.int32, (share, width), 0)
        j = lax.broadcasted_iota(jnp.int32, (share, width), 1) % columns
        shift = jnp.where(row < edge, tap_first % TAPS, tap_next % TAPS) - 1

        def right_of(move):
            return maps[:, pl.ds(1 + start + move, depth)].reshape(width, channels)

        both = jnp.concatenate(
            [right_of(tap_first // TAPS - 1), right_of(tap_next // TAPS - 1)], axis=1
        )
        picked = lax.dot_general(
            select, both, (((1,), (1,)), ((), ())), preferred_element_type=jnp.float32
        )

        def lower(value):
            return jnp.where(j < columns - 1, pltpu.roll(value, width - 1, 1), 0.0)

        def higher(value):
            return jnp.where(j > 0, pltpu.roll(value, 1, 1), 0.0)

        left = jnp.where(
            shift == 0, picked, jnp.where(shift > 0, lower(picked), higher(picked))
        )
        stacked = jnp.concatenate([lower(left), left, higher(left)], axis=0).astype(maps.dtype)
        for ky in range(TAPS):
            part = jnp.dot(stacked, right_of(ky - 1), preferred_element_type=jnp.float32)
            for kx in range(TAPS):
                at = (TAPS * ky + kx) * channels
                piece = part[kx * share : (kx + 1) * share]
                if fresh[0]:
                    sums[:, at : at + channels] = piece
                else:
                    sums[:, at : at + channels] += piece
        fresh[0] = False

    fresh = [True]
    line_rows = 4 * rows
    side = line_rows + line_rows // 2
    forward_first(2)
    forward_second(1)
    forward_first(3)
    grad_copies = []
    for n, line in enumerate(order):
        for m, yy in enumerate((y, y_other)):
            if n == 0 and m == 0:
                continue
            index = 2 * n + m
            one = copy(gpart.at[place(line, yy, core)], grecv.at[2 * z + y],
                       ss.at[index], rs.at[2 * z + y], (x, place(line, yy, core)))
            one.start()
            got = copy(gpart.at[place(line, yy, core)], grecv.at[2 * line + yy],
                       ss.at[index], rs.at[2 * line + yy], (x, place(line, yy, core)))
            grad_copies.append((one, got))

    forward_second(2)
    wait_partner(0)
    wait_partner(1)
    stage(half * (height - side), side)
    forward_second(3)
    wait_partner(2)
    stage(side, height - 2 * side)
    wait_partner(3)
    stage((1 - half) * (height - side), side)

    total = gpart[space]
    for one, got in grad_copies:
        got.wait_recv()
    for n, line in enumerate(order):
        for m, yy in enumerate((y, y_other)):
            if n == 0 and m == 0:
                continue
            total = total + grecv[2 * line + yy]
    grad_sum[...] = total

    for one, got in grad_copies:
        one.wait_send()
    for one in x_copy + y_copy + dx_copy + dy_copy + [z_near, gx, gp0, gp1]:
        one.wait_send()

    @pl.when(is_middle)
    def _():
        z_across.wait_send()
        for n in z_pass:
            z_pass[n].wait_send()

    for pair in p_copy:
        pair[0].wait_send()
        pair[1].wait_send()


def kernel_form(activations, out_grads, old_input_factor, old_grad_factor):
    images, rows, columns, channels = activations.shape
    groups = lax.axis_size("dp")
    spaces = lax.axis_size("space")
    lines = spaces // 4
    height = rows * spaces
    positions = images * groups * height * columns
    share, width_all = old_input_factor.shape
    grad_share = old_grad_factor.shape[0]
    dma = pltpu.SemaphoreType.DMA
    vmem = pl.BlockSpec(memory_space=pltpu.VMEM)
    hbm = pl.BlockSpec(memory_space=pltpu.HBM)
    input_sum, grad_sum = pl.pallas_call(
        gather_kernel,
        out_shape=(
            jax.ShapeDtypeStruct((share, width_all), jnp.float32),
            jax.ShapeDtypeStruct((grad_share, channels), jnp.float32),
        ),
        in_specs=[hbm, hbm],
        out_specs=(vmem, vmem),
        scratch_shapes=[
            pltpu.VMEM((images * groups, height + 2, columns, channels), activations.dtype),
            pltpu.VMEM((4,) + out_grads.shape, out_grads.dtype),
            pltpu.VMEM((spaces, grad_share, channels), jnp.float32),
            pltpu.VMEM((2 * lines, grad_share, channels), jnp.float32),
        ]
        + [dma((2,))]
        + [dma((lines + 1,)), dma((lines,))]
        + [dma((lines,))] * 8
        + [dma((lines, 2))] * 2
        + [dma((3,))] * 2
        + [dma((2 * lines,))] * 2,
        compiler_params=pltpu.CompilerParams(
            collective_id=0, has_side_effects=True, vmem_limit_bytes=24 * 2**20
        ),
        cost_estimate=pl.CostEstimate(
            flops=2 * positions * share * width_all, bytes_accessed=4 * share * width_all,
            transcendentals=0,
        ),
    )(activations, out_grads)
    input_factor = 0.5 * old_input_factor.astype(jnp.float32) + 0.5 / positions * input_sum
    grad_factor = 0.5 * old_grad_factor + 0.5 / positions * grad_sum
    return input_factor, grad_factor


def per_device(activations, out_grads, old_input_factor, old_grad_factor):
    groups, spaces = lax.axis_size("dp"), lax.axis_size("space")
    images, channels = activations.shape[0], activations.shape[3]
    whole_map = activations.size * groups * spaces
    small = whole_map <= old_input_factor.shape[1] ** 2
    fits = groups == 2 and spaces == 16 and images % 2 == 0 and old_input_factor.shape[0] <= channels
    form = kernel_form if small and fits else reduced_form
    return form(activations, out_grads, old_input_factor, old_grad_factor)


def solution(mesh):
    return jax.shard_map(
        per_device,
        mesh=mesh,
        in_specs=(
            P("dp", "space", None, None),
            P("dp", "space", None, None),
            P(("dp", "space"), None),
            P("space", None),
        ),
        out_specs=(P(("dp", "space"), None), P("space", None)),
        check_vma=False,
    )
```
